32 devices in a mesh: grp: 2 (over x), exp: 16 (over z, y, core).
Axes of the slice: x: 2, y: 2, z: 4, core: 2. Of those that a mesh axis runs over, the one named last changes fastest.
Arguments:
- tokens: bfloat16 [512, 4096], P(('grp', 'exp')), parts along dimension 0, may hold values from -6 to 6
- norm_gain: float32 [4096], replicated, may hold values from 0.1 to 1.9
- gate_weight: bfloat16 [4096, 24576], P(None, 'exp'), may hold values from -0.09375 to 0.09375
- up_weight: bfloat16 [4096, 24576], P(None, 'exp'), may hold values from -0.09375 to 0.09375
- down_weight: bfloat16 [24576, 4096], P('exp'), may hold values from -0.15625 to 0.15625
- routes: int32 [512, 8], P(('grp', 'exp')), parts along dimension 0, may hold values from 0 to 15, all different within a row; in each aligned block of 16 rows (0 to 15, 16 to 31, ...) at most 9 rows name the same one
- fractions: int32 [512, 8], P(('grp', 'exp')), parts along dimension 0, may hold values from 1 to 16
- cotangent: bfloat16 [512, 4096], P(('grp', 'exp')), parts along dimension 0, may hold values from -6 to 6
Outputs:
- mixed: bfloat16 [512, 4096], P(('grp', 'exp')), parts along dimension 0
- token_grad: bfloat16 [512, 4096], P(('grp', 'exp')), parts along dimension 0
The draws below stay inside these ranges and needn't reach their ends.
There are 2 independent parts, one for each index of `grp`. The reference program is written for one: setup_inputs(seed, part) draws one part's arguments, and reference() takes and returns one part's arrays. A program takes and returns all parts, laid end to end along the dimension named above; an argument that names none is the same for every part. Nothing has to cross between parts.
Inputs may be any that keep to these rules, and one draw needn't show every extreme that they name: `routes`: each row names 8 different experts. Among the 16 rows of one device, at most 9 name one expert, a bound that some block reaches of them.
All inputs are finite; a program needn't handle non-finite values.
Results may differ from the reference program's by a relative error of at most 0.0071.
Values may be sent and summed in bfloat16 or wider, within the bound.
A program may use at most 128 MiB of HBM per device.

```python
import math
import jax
import jax.numpy as jnp
import numpy as np
from jax import lax

D = 4096
FF = 1536
TOP = 8
EXPERTS = 16
TOK_DEV = 16
CAP = 9
TOKENS = 256
N_EXP = 16


def place_ends(entries, stream_key, low, top_value):
    place = [jax.random.randint(jax.random.fold_in(stream_key, axis), (), 0, length) for axis, length in enumerate(entries.shape)]
    main_axis = entries.shape.index(max(entries.shape))
    next_to = place[:main_axis] + [(place[main_axis] + 1) % entries.shape[main_axis]] + place[main_axis + 1:]
    return entries.at[tuple(place)].set(low).at[tuple(next_to)].set(top_value)


def levels(own_key, shape, split, least, largest):
    factor_of, own = 1.0, jax.random.fold_in(own_key, 6)
    for dim, shards_of in split:
        draws = jnp.exp(jax.random.uniform(jax.random.fold_in(own, dim), (shards_of,), jnp.float32, least / len(split), largest / len(split)))
        factor_of = factor_of * jnp.repeat(draws, shape[dim] // shards_of).reshape([-1 if axis == dim else 1 for axis in range(len(shape))])
    return factor_of


def routed_block(rng, own, number, rows, number_of, top, most, skew):
    ranking = jax.random.permutation(rng, number_of)
    heavy_load, common = load_shares(number_of, rows * top, most, skew, True), load_shares(number_of, rows * top, most, skew, False)
    places = jnp.arange(number_of)

    def named(sizes, turn):
        used = int((sizes > 0).sum())
        fixed = max(1, used // 4)
        moved = fixed + (places - fixed + turn * (used - fixed)) % max(1, number_of - fixed)
        return jnp.zeros((number_of,), jnp.int32).at[ranking[jnp.where(places < fixed, places, moved)]].set(jnp.asarray(sizes, jnp.int32))

    sizes = jnp.where(number % 4 == 0, named(heavy_load, number // 4), named(common, number - number // 4 - 1))
    mixed = jax.random.permutation(jax.random.fold_in(own, 3), number_of)
    giver, taker = mixed[0:number_of // 2 * 2:2], mixed[1:number_of // 2 * 2:2]
    slack = jnp.minimum(sizes[giver] - 1, most - sizes[taker]) // 2
    slack = jnp.where((giver == ranking[0]) | (taker == ranking[0]) | (sizes[taker] == 0), 0, jnp.maximum(slack, 0))
    moved = jax.random.randint(jax.random.fold_in(own, 4), (number_of // 2,), 0, 1 << 20) % (slack + 1)
    sizes = sizes.at[giver].add(-moved).at[taker].add(moved)
    labels = jnp.searchsorted(jnp.cumsum(sizes), jnp.arange(rows * top), side="right").astype(jnp.int32)
    grid = labels.reshape(top, rows).T
    grid = grid[jax.random.permutation(jax.random.fold_in(own, 1), rows)]
    turn = jax.random.randint(jax.random.fold_in(own, 2), (rows, 1), 0, top)
    return jnp.take_along_axis(grid, (jnp.arange(top)[None, :] + turn) % top, axis=1)


def load_shares(amount, total, limit, lean, full):
    portions = [(1 << 20) // math.isqrt(standing ** lean) + 1 for standing in range(1, amount + 1)]
    largest = limit if full else min(limit, max(-(-total // amount), total * portions[0] // sum(portions)))
    least = 1 if total - largest >= amount - 1 else 0
    counts, rest = [largest] + [least] * (amount - 1), total - largest - least * (amount - 1)
    while rest > 0:
        free = [i for i in range(1, amount) if counts[i] < largest] or [i for i in range(1, amount) if counts[i] < limit]
        pool, remaining = sum([portions[i] for i in free]), rest
        for i in free:
            extra = min(limit - counts[i], max(1, remaining * portions[i] // pool), rest)
            counts[i] = counts[i] + extra
            rest = rest - extra
    return np.array(counts)


def centred(rng, dims, deviation, most, cuts=(), dtype=jnp.bfloat16):
    array = deviation * jax.random.normal(rng, dims, jnp.float32)
    if cuts:
        array = array * levels(rng, dims, cuts, -0.22, 0.18)
    return jnp.clip(array, -most, most).astype(dtype)


def setup_inputs(seed: int = 0, part: int = 0) -> dict:
    keys = jax.random.split(jax.random.key(seed), 9)
    part_splits = jax.random.split(jax.random.fold_in(keys[8], part), 9)
    tokens = centred(part_splits[0], (TOKENS, D), 1.0, 6.0, ((0, 16),))
    norm_gain = jnp.clip(1.0 + 0.18 * jax.random.normal(keys[1], (D,), jnp.float32), 0.1, 1.9)
    gate_weight = centred(keys[2], (D, EXPERTS * FF), D ** -0.5, 0.09375, ((1, 16),))
    up_weight = centred(keys[3], (D, EXPERTS * FF), D ** -0.5, 0.09375, ((1, 16),))
    down_weight = centred(keys[4], (EXPERTS * FF, D), FF ** -0.5, 0.15625, ((0, 16),))
    routes_keys = jax.random.split(jax.random.fold_in(part_splits[5], 1), TOKENS // TOK_DEV)
    routes_turns = jax.random.permutation(jax.random.fold_in(part_splits[5], 3), TOKENS // TOK_DEV)
    routes = jax.vmap(lambda own, number: routed_block(jax.random.fold_in(part_splits[5], 2), own, number, TOK_DEV, EXPERTS, TOP, CAP, 2))(routes_keys, routes_turns).reshape((TOKENS, TOP))
    fractions = place_ends(jax.random.randint(part_splits[6], (TOKENS, TOP), 1, 17), jax.random.fold_in(part_splits[6], 1), 1, 16).astype(jnp.int32)
    cotangent = centred(part_splits[7], (TOKENS, D), 1.0, 6.0, ((0, 16),))
    return dict(tokens=tokens, norm_gain=norm_gain, gate_weight=gate_weight, up_weight=up_weight, down_weight=down_weight, routes=routes, fractions=fractions, cotangent=cotangent)


def normalize(values, gain):
    scale = lax.rsqrt(lax.optimization_barrier(jnp.mean(values * values, axis=-1, keepdims=True)) + 1e-06)
    return values * scale * gain

def settle(values):
    return lax.optimization_barrier(values.astype(jnp.bfloat16)).astype(jnp.float32)

def expert_pass(rows, grads, w_gate, w_up, w_down, blocks):
    gate = jnp.dot(rows, w_gate, preferred_element_type=jnp.float32)
    upper = jnp.dot(rows, w_up, preferred_element_type=jnp.float32)
    sigma = jax.nn.sigmoid(gate)
    silu_gate = gate * sigma
    act = (silu_gate * upper).astype(jnp.bfloat16)
    dact = jnp.dot(grads, w_down.T, preferred_element_type=jnp.float32)
    dgate = (dact * upper * sigma * (1.0 + gate * (1.0 - sigma))).astype(jnp.bfloat16)
    dup = (dact * silu_gate).astype(jnp.bfloat16)
    span = w_gate.shape[1] // blocks
    output = jnp.zeros((rows.shape[0], w_down.shape[1]), jnp.float32)
    backed = jnp.zeros((rows.shape[0], w_gate.shape[0]), jnp.float32)
    for block in range(blocks):
        low = block * span
        high = low + span
        piece_out = jnp.dot(act[:, low:high], w_down[low:high, :], preferred_element_type=jnp.float32)
        piece_back = jnp.dot(dgate[:, low:high], w_gate[:, low:high].T, preferred_element_type=jnp.float32)
        piece_back = piece_back + jnp.dot(dup[:, low:high], w_up[:, low:high].T, preferred_element_type=jnp.float32)
        output = output + settle(piece_out)
        backed = backed + settle(piece_back)
    return (output, backed)

def reference(tokens, norm_gain, gate_weight, up_weight, down_weight, routes, fractions, cotangent):
    blocks = N_EXP // EXPERTS
    values = tokens.astype(jnp.float32)
    normed, pullback = jax.vjp(lambda v: normalize(v, norm_gain), values)
    normed_b = normed.astype(jnp.bfloat16)
    shares = fractions.astype(jnp.float32)
    shares = shares / lax.optimization_barrier(jnp.sum(shares, axis=-1, keepdims=True))

    def step(expert, carry):
        total_out, total_back = carry
        mine = lax.optimization_barrier(jnp.sum(jnp.where(routes == expert, shares, jnp.float32(0.0)), axis=1))
        start = (expert * FF).astype(jnp.int32)
        w_gate = lax.dynamic_slice_in_dim(gate_weight, start, FF, 1)
        w_up = lax.dynamic_slice_in_dim(up_weight, start, FF, 1)
        w_down = lax.dynamic_slice_in_dim(down_weight, start, FF, 0)
        output, backed = expert_pass(normed_b, cotangent, w_gate, w_up, w_down, blocks)
        output = settle(output)
        backed = settle(backed)
        return (total_out + mine[:, None] * output, total_back + mine[:, None] * backed)
    zeros = jnp.zeros(values.shape, jnp.float32)
    total_out, total_back = lax.fori_loop(jnp.int32(0), jnp.int32(EXPERTS), step, (zeros, zeros))
    token_grad = pullback(total_back)[0]
    return (total_out.astype(jnp.bfloat16), token_grad.astype(jnp.bfloat16))
```

```python
import functools

import jax
import jax.numpy as jnp
from jax import lax
from jax.experimental import pallas as pl
from jax.experimental.pallas import tpu as pltpu
from jax.sharding import PartitionSpec as P

EXPERTS = 16
LANES = 128
LEAD = 2
MESH = pl.DeviceIdType.MESH
F32 = jnp.float32
BF16 = jnp.bfloat16


def dot(a, b):
    return lax.dot_general(a, b, (((1,), (0,)), ((), ())), preferred_element_type=F32)


def dot_t(a, b):
    return lax.dot_general(a, b, (((1,), (1,)), ((), ())), preferred_element_type=F32)


def kernel(
    nz,
    ny,
    chunks,
    tokens,
    gain,
    routes,
    fractions,
    cotangent,
    w_gate,
    w_up,
    w_down,
    mixed,
    token_grad,
    data,
    gate_v,
    up_v,
    down_v,
    gate,
    upper,
    dact,
    act,
    dgate,
    dup,
    from_core,
    from_y,
    from_z,
    final,
    w_sem,
    zs,
    zr,
    ys,
    yr,
    cs,
    cr,
    a_s,
    a_r,
    b_s,
    b_r,
    ps,
    pr,
):
    rows, width = tokens.shape
    cols = width // chunks
    hidden = w_gate.shape[1]
    total = 2 * ny * nz * rows
    me = lax.axis_index("exp")
    c = lax.rem(me, 2)
    y = lax.rem(me // 2, ny)
    z = me // (2 * ny)

    def at(zz, yy, cc):
        return (zz * ny + yy) * 2 + cc

    sibling = at(z, y, 1 - c)
    across = at(z, ny - 1 - y, c)
    ahead = at(z + 1, y, c)
    behind = at(z - 1, y, c)

    def weights(q):
        part = pl.ds(q * cols, cols)
        return (
            pltpu.make_async_copy(w_gate.at[part, :], gate_v.at[q], w_sem.at[q, 0]),
            pltpu.make_async_copy(w_up.at[part, :], up_v.at[q], w_sem.at[q, 1]),
            pltpu.make_async_copy(w_down.at[:, part], down_v.at[q], w_sem.at[q, 2]),
        )

    barrier = pltpu.get_barrier_semaphore()

    def greet(device):
        pl.semaphore_signal(barrier, inc=1, device_id={"exp": device}, device_id_type=MESH)

    greet(sibling)
    if ny > 1:
        greet(across)
    pl.when(z + 1 < nz)(lambda: greet(ahead))
    pl.when(z > 0)(lambda: greet(behind))

    for q in range(chunks):
        for copy in weights(q):
            copy.start()

    values = tokens[...].astype(F32)
    scale = lax.rsqrt(jnp.mean(values * values, axis=-1, keepdims=True) + 1e-06)
    normed = (values * scale * gain[...]).astype(BF16)
    own = pl.ds(pl.multiple_of(((c * ny + y) * nz + z) * rows, rows), rows)
    lane = lax.broadcasted_iota(jnp.int32, (rows, LANES), 1)
    table = jnp.zeros((rows, LANES), F32)
    for k in range(routes.shape[1]):
        table = table + jnp.where(
            routes[:, k : k + 1] == lane, fractions[:, k : k + 1].astype(F32), 0.0
        )
    data[0, own, 2 * cols :] = table.astype(BF16)
    for q in range(chunks):
        data[q, own, :cols] = normed[:, q * cols : (q + 1) * cols]
        data[q, own, cols : 2 * cols] = cotangent[:, q * cols : (q + 1) * cols]

    peers = jnp.int32(2 if ny > 1 else 1) + (z + 1 < nz).astype(jnp.int32) + (z > 0).astype(jnp.int32)
    pl.semaphore_wait(barrier, peers)

    def span(q):
        return 2 * cols + (LANES if q == 0 else 0)

    def place(cc, yy, zz):
        return pl.multiple_of(((cc * ny + yy) * nz + zz) * rows, rows)

    def held(q, cc, yy, zz, count=1, columns=None):
        return data.at[
            q, pl.ds(place(cc, yy, zz), count * rows), pl.ds(0, span(q) if columns is None else columns)
        ]

    def remote(src, dst, send, recv, device):
        return pltpu.make_async_remote_copy(
            src_ref=src,
            dst_ref=dst,
            send_sem=send,
            recv_sem=recv,
            device_id={"exp": device},
            device_id_type=MESH,
        )

    def z_copy(q, way, hop, block):
        ref = held(q, c, y, block)
        return remote(
            ref, ref, zs.at[q, way, hop - 1], zr.at[q, way, hop - 1], ahead if way == 0 else behind
        )

    def z_sends(q, hop, act_on):
        pl.when((z + 1 < nz) & (z >= hop - 1))(lambda: act_on(z_copy(q, 0, hop, z - hop + 1)))
        pl.when((z > 0) & (z + hop - 1 < nz))(lambda: act_on(z_copy(q, 1, hop, z + hop - 1)))

    def y_copy(q, block, yy):
        ref = held(q, c, yy, block)
        return remote(ref, ref, ys.at[q, block], yr.at[q, block], across)

    def c_copy(q, cc, half):
        ref = held(q, cc, y if half == 0 else ny - 1 - y, 0, nz)
        return remote(ref, ref, cs.at[q, half], cr.at[q, half], sibling)

    def begin(q):
        z_sends(q, 1, lambda copy: copy.start())
        if ny > 1:
            y_copy(q, z, y).start()

    def gather_hop(q, hop):
        def arrived(way, block):
            z_copy(q, way, hop, block).wait_recv()
            if ny > 1:
                y_copy(q, block, y).start()

        pl.when(z >= hop)(lambda: arrived(0, z - hop))
        pl.when(z + hop < nz)(lambda: arrived(1, z + hop))
        if hop < nz - 1:
            z_sends(q, hop + 1, lambda copy: copy.start())
        else:
            c_copy(q, c, 0).start()

    def gather_across(q):
        if ny > 1:
            for block in range(nz):
                y_copy(q, block, ny - 1 - y).wait_recv()
            c_copy(q, c, 1).start()

    step = 256 if total % 256 == 0 else total
    tile = 256 if hidden % 256 == 0 else LANES

    def first(q):
        c_copy(q, 1 - c, 0).wait_recv()
        if ny > 1:
            c_copy(q, 1 - c, 1).wait_recv()
        for copy in weights(q):
            copy.wait()
        for low in range(0, total, step):
            some = slice(low, low + step)

            @pl.loop(0, hidden // tile)
            def _(n):
                part = pl.ds(pl.multiple_of(n * tile, tile), tile)
                x = data[q, some, :cols]
                g = dot(x, gate_v[q, :, part])
                u = dot(x, up_v[q, :, part])
                d = dot_t(data[q, some, cols : 2 * cols], down_v[q, part, :])
                if q == 0:
                    gate[some, part] = g
                    upper[some, part] = u
                    dact[some, part] = d
                else:
                    gate[some, part] += g
                    upper[some, part] += u
                    dact[some, part] += d

    for q in range(min(LEAD, chunks)):
        begin(q)
    for slot in range(chunks + nz + 1):
        if LEAD <= slot + LEAD < chunks:
            begin(slot + LEAD)
        for stage in range(nz, 0, -1):
            q = slot - stage + 1
            if 0 <= q < chunks:
                if stage < nz:
                    gather_hop(q, stage)
                else:
                    gather_across(q)
        if 0 <= slot - nz < chunks:
            first(slot - nz)

    for q in range(chunks):
        for hop in range(1, nz):
            z_sends(q, hop, lambda copy: copy.wait_send())
        if ny > 1:
            for block in range(nz):
                y_copy(q, block, y).wait_send()
            c_copy(q, c, 1).wait_send()
        c_copy(q, c, 0).wait_send()

    mine = me // (2 * ny * nz // EXPERTS)
    for low in range(0, total, step):
        some = slice(low, low + step)
        named = data[0, some, 2 * cols :].astype(F32)
        lanes = lax.broadcasted_iota(jnp.int32, named.shape, 1)
        share = jnp.sum(jnp.where(lanes == mine, named, 0.0), axis=1, keepdims=True)
        share = share / jnp.sum(named, axis=1, keepdims=True)

        @pl.loop(0, hidden // LANES)
        def _(n):
            part = pl.ds(pl.multiple_of(n * LANES, LANES), LANES)
            g = gate[some, part]
            u = upper[some, part]
            d = dact[some, part] * share
            sigma = jax.nn.sigmoid(g)
            silu = g * sigma
            act[some, part] = (silu * u * share).astype(BF16)
            dgate[some, part] = (d * u * sigma * (1.0 + g * (1.0 - sigma))).astype(BF16)
            dup[some, part] = (d * silu).astype(BF16)

    def a_copy(q):
        return remote(
            held(q, 1 - c, 0, 0, ny * nz, 2 * cols), from_core.at[q], a_s.at[q], a_r.at[q], sibling
        )

    def b_copy(q):
        return remote(
            held(q, c, ny - 1 - y, 0, nz, 2 * cols), from_y.at[q], b_s.at[q], b_r.at[q], across
        )

    def landing(q, way, block):
        return from_z.at[q, pl.ds(pl.multiple_of((block + 1 - way) * rows, rows), rows), :]

    def p_copy(q, way, hop, block):
        return remote(
            held(q, c, y, block, 1, 2 * cols),
            landing(q, way, block),
            ps.at[q, way, hop - 1],
            pr.at[q, way, hop - 1],
            ahead if way == 0 else behind,
        )

    def p_sends(q, hop, act_on):
        pl.when(z < hop)(lambda: act_on(p_copy(q, 0, hop, z + nz - hop)))
        pl.when(nz - 1 - z < hop)(lambda: act_on(p_copy(q, 1, hop, z - nz + hop)))

    wide = 256 if cols % 256 == 0 else LANES

    def second(q):
        for low in range(0, total, step):
            some = slice(low, low + step)

            @pl.loop(0, cols // wide)
            def _(n):
                start = pl.multiple_of(n * wide, wide)
                part = pl.ds(start, wide)
                out = dot(act[some, :], down_v[q, :, part])
                back = dot_t(dgate[some, :], gate_v[q, part, :])
                back = back + dot_t(dup[some, :], up_v[q, part, :])
                data[q, some, part] = out.astype(BF16)
                data[q, some, pl.ds(pl.multiple_of(cols + start, LANES), wide)] = back.astype(BF16)

        a_copy(q).start()

    def add(q, start, count, other):
        ref = data.at[q, pl.ds(start, count), pl.ds(0, 2 * cols)]
        ref[...] = (ref[...].astype(F32) + other.astype(F32)).astype(BF16)

    def sum_core(q):
        a_copy(q).wait_recv()
        if ny > 1:
            theirs = (ny - 1 - y) * nz * rows
            add(q, place(c, ny - 1 - y, 0), nz * rows, from_core[q, pl.ds(pl.multiple_of(theirs, rows), nz * rows), :])
            b_copy(q).start()
        add(q, place(c, y, 0), nz * rows, from_core[q, pl.ds(pl.multiple_of(y * nz * rows, rows), nz * rows), :])

    def sum_across(q):
        if ny > 1:
            b_copy(q).wait_recv()
            add(q, place(c, y, 0), nz * rows, from_y[q])
        p_sends(q, 1, lambda copy: copy.start())

    def sum_hop(q, hop):
        def arrived(way, block):
            p_copy(q, way, hop, block).wait_recv()
            if hop < nz - 1:
                add(q, place(c, y, block), rows, landing(q, way, block)[...])

        pl.when((z > 0) & (z - 1 < hop))(lambda: arrived(0, z - 1 + nz - hop))
        pl.when((z + 1 < nz) & (nz - 2 - z < hop))(lambda: arrived(1, z + 1 - nz + hop))
        if hop < nz - 1:
            p_sends(q, hop + 1, lambda copy: copy.start())
            return
        part = slice(q * 2 * cols, (q + 1) * 2 * cols)
        final[:, part] = held(q, c, y, z, 1, 2 * cols)[...].astype(F32)

        @pl.when(z > 0)
        def _():
            final[:, part] += landing(q, 0, z)[...].astype(F32)

        @pl.when(z + 1 < nz)
        def _():
            final[:, part] += landing(q, 1, z)[...].astype(F32)

    for slot in range(chunks + nz + 1):
        if slot < chunks:
            second(slot)
        for stage in range(nz + 1, 0, -1):
            q = slot - stage
            if 0 <= q < chunks:
                if stage == 1:
                    sum_core(q)
                elif stage == 2:
                    sum_across(q)
                else:
                    sum_hop(q, stage - 2)

    for q in range(chunks):
        a_copy(q).wait_send()
        if ny > 1:
            b_copy(q).wait_send()
        for hop in range(1, nz):
            p_sends(q, hop, lambda copy: copy.wait_send())

    values = tokens[...].astype(F32)
    scale = lax.rsqrt(jnp.mean(values * values, axis=-1, keepdims=True) + 1e-06)
    inner = jnp.zeros((rows, 1), F32)
    for q in range(chunks):
        part = slice(q * cols, (q + 1) * cols)
        mixed[:, part] = final[:, 2 * q * cols : (2 * q + 1) * cols].astype(BF16)
        scaled = final[:, (2 * q + 1) * cols : (2 * q + 2) * cols] * gain[:, part]
        final[:, (2 * q + 1) * cols : (2 * q + 2) * cols] = scaled
        inner = inner + jnp.sum(scaled * values[:, part], axis=-1, keepdims=True)
    inner = inner / width * scale * scale * scale
    for q in range(chunks):
        part = slice(q * cols, (q + 1) * cols)
        scaled = final[:, (2 * q + 1) * cols : (2 * q + 2) * cols]
        token_grad[:, part] = (scaled * scale - values[:, part] * inner).astype(BF16)


def local(nz, ny, tokens, norm_gain, gate_weight, up_weight, down_weight, routes, fractions, cotangent):
    rows, width = tokens.shape
    hidden = gate_weight.shape[1]
    chunks = max(1, 32 // nz)
    cols = width // chunks
    total = 2 * ny * nz * rows
    dma = pltpu.SemaphoreType.DMA
    in_vmem = pl.BlockSpec(memory_space=pltpu.VMEM)
    in_hbm = pl.BlockSpec(memory_space=pl.ANY)
    out = jax.ShapeDtypeStruct((rows, width), BF16)
    hops = max(1, nz - 1)
    return pl.pallas_call(
        functools.partial(kernel, nz, ny, chunks),
        out_shape=(out, out),
        in_specs=[in_vmem] * 5 + [in_hbm] * 3,
        out_specs=(in_vmem, in_vmem),
        scratch_shapes=[
            pltpu.VMEM((chunks, total, 2 * cols + LANES), BF16),
            pltpu.VMEM((chunks, cols, hidden), BF16),
            pltpu.VMEM((chunks, cols, hidden), BF16),
            pltpu.VMEM((chunks, hidden, cols), BF16),
            pltpu.VMEM((total, hidden), F32),
            pltpu.VMEM((total, hidden), F32),
            pltpu.VMEM((total, hidden), F32),
            pltpu.VMEM((total, hidden), BF16),
            pltpu.VMEM((total, hidden), BF16),
            pltpu.VMEM((total, hidden), BF16),
            pltpu.VMEM((chunks, total // 2, 2 * cols), BF16),
            pltpu.VMEM((chunks, nz * rows if ny > 1 else 16, 2 * cols), BF16),
            pltpu.VMEM((chunks, (nz + 1) * rows, 2 * cols), BF16),
            pltpu.VMEM((rows, 2 * width), F32),
            dma((chunks, 3)),
            dma((chunks, 2, hops)),
            dma((chunks, 2, hops)),
            dma((chunks, nz)),
            dma((chunks, nz)),
            dma((chunks, 2)),
            dma((chunks, 2)),
            dma((chunks,)),
            dma((chunks,)),
            dma((chunks,)),
            dma((chunks,)),
            dma((chunks, 2, hops)),
            dma((chunks, 2, hops)),
        ],
        compiler_params=pltpu.CompilerParams(
            collective_id=0, has_side_effects=True, vmem_limit_bytes=62 * 1024 * 1024
        ),
        cost_estimate=pl.CostEstimate(
            flops=12 * total * width * hidden,
            bytes_accessed=6 * width * hidden,
            transcendentals=total * hidden,
        ),
    )(tokens, norm_gain.reshape(1, width), routes, fractions, cotangent, gate_weight, up_weight, down_weight)


def solution(mesh):
    rows = P(("grp", "exp"), None)
    placed = (rows, P(), P(None, "exp"), P(None, "exp"), P("exp", None), rows, rows, rows)
    ny = max(1, 4 // mesh.shape["grp"])
    nz = mesh.shape["exp"] // (2 * ny)
    return jax.shard_map(
        functools.partial(local, nz, ny),
        mesh=mesh,
        in_specs=placed,
        out_specs=(rows, rows),
        check_vma=False,
    )
```

```python
import functools

import jax
import jax.numpy as jnp
from jax import lax
from jax.experimental import pallas as pl
from jax.experimental.pallas import tpu as pltpu
from jax.sharding import PartitionSpec as P

EXPERTS = 16
LANES = 128
LEAD = 2
GAP = 2
MESH = pl.DeviceIdType.MESH
F32 = jnp.float32
BF16 = jnp.bfloat16


def dot(a, b):
    return lax.dot_general(a, b, (((1,), (0,)), ((), ())), preferred_element_type=F32)


def dot_t(a, b):
    return lax.dot_general(a, b, (((1,), (1,)), ((), ())), preferred_element_type=F32)


def kernel(
    nz,
    ny,
    chunks,
    tokens,
    gain,
    routes,
    fractions,
    cotangent,
    w_gate,
    w_up,
    w_down,
    mixed,
    token_grad,
    data,
    gate_v,
    up_v,
    down_v,
    gate,
    upper,
    dact,
    act,
    dgate,
    dup,
    from_core,
    from_y,
    from_z,
    final,
    w_sem,
    zs,
    zr,
    ys,
    yr,
    cs,
    cr,
    a_s,
    a_r,
    b_s,
    b_r,
    ps,
    pr,
):
    rows, width = tokens.shape
    cols = width // chunks
    hidden = w_gate.shape[1]
    total = 2 * ny * nz * rows
    me = lax.axis_index("exp")
    c = lax.rem(me, 2)
    y = lax.rem(me // 2, ny)
    z = me // (2 * ny)

    def at(zz, yy, cc):
        return (zz * ny + yy) * 2 + cc

    sibling = at(z, y, 1 - c)
    across = at(z, ny - 1 - y, c)
    def weights(q):
        part = pl.ds(q * cols, cols)
        return (
            pltpu.make_async_copy(w_gate.at[part, :], gate_v.at[q], w_sem.at[q, 0]),
            pltpu.make_async_copy(w_up.at[part, :], up_v.at[q], w_sem.at[q, 1]),
            pltpu.make_async_copy(w_down.at[:, part], down_v.at[q], w_sem.at[q, 2]),
        )

    barrier = pltpu.get_barrier_semaphore()

    def greet(device):
        pl.semaphore_signal(barrier, inc=1, device_id={"exp": device}, device_id_type=MESH)

    greet(sibling)
    if ny > 1:
        greet(across)
    peers = (2 if ny > 1 else 1) + nz - 1
    for offset in range(1, nz):
        greet(at(lax.rem(z + offset, nz), y, c))

    for q in range(chunks):
        for copy in weights(q):
            copy.start()

    values = tokens[...].astype(F32)
    scale = lax.rsqrt(jnp.mean(values * values, axis=-1, keepdims=True) + 1e-06)
    normed = (values * scale * gain[...]).astype(BF16)
    own = pl.ds(pl.multiple_of(((c * ny + y) * nz + z) * rows, rows), rows)
    lane = lax.broadcasted_iota(jnp.int32, (rows, LANES), 1)
    table = jnp.zeros((rows, LANES), F32)
    for k in range(routes.shape[1]):
        table = table + jnp.where(
            routes[:, k : k + 1] == lane, fractions[:, k : k + 1].astype(F32), 0.0
        )
    data[0, own, 2 * cols :] = table.astype(BF16)
    for q in range(chunks):
        data[q, own, :cols] = normed[:, q * cols : (q + 1) * cols]
        data[q, own, cols : 2 * cols] = cotangent[:, q * cols : (q + 1) * cols]

    pl.semaphore_wait(barrier, peers)

    def span(q):
        return 2 * cols + (LANES if q == 0 else 0)

    def place(cc, yy, zz):
        return pl.multiple_of(((cc * ny + yy) * nz + zz) * rows, rows)

    def held(q, cc, yy, zz, count=1, columns=None):
        return data.at[
            q, pl.ds(place(cc, yy, zz), count * rows), pl.ds(0, span(q) if columns is None else columns)
        ]

    def remote(src, dst, send, recv, device):
        return pltpu.make_async_remote_copy(
            src_ref=src,
            dst_ref=dst,
            send_sem=send,
            recv_sem=recv,
            device_id={"exp": device},
            device_id_type=MESH,
        )

    def both(offset, visit):
        pl.when(z + offset < nz)(lambda: visit(0, z + offset))
        pl.when(z >= offset)(lambda: visit(1, z - offset))

    def z_copy(q, way, offset, block, other):
        ref = held(q, c, y, block)
        return remote(
            ref, ref, zs.at[q, way, offset - 1], zr.at[q, way, offset - 1], at(other, y, c)
        )

    def y_copy(q, block, yy):
        ref = held(q, c, yy, block)
        return remote(ref, ref, ys.at[q, block], yr.at[q, block], across)

    def c_copy(q, cc, half):
        ref = held(q, cc, y if half == 0 else ny - 1 - y, 0, nz)
        return remote(ref, ref, cs.at[q, half], cr.at[q, half], sibling)

    def begin(q):
        for offset in range(1, nz):
            both(offset, lambda way, other: z_copy(q, way, offset, z, other).start())
        if ny > 1:
            y_copy(q, z, y).start()

    def gather_z(q):
        def arrived(way, offset, other):
            z_copy(q, 1 - way, offset, other, other).wait_recv()
            if ny > 1:
                y_copy(q, other, y).start()

        for offset in range(1, nz):
            both(offset, lambda way, other: arrived(way, offset, other))
        c_copy(q, c, 0).start()

    def gather_across(q):
        if ny > 1:
            for block in range(nz):
                y_copy(q, block, ny - 1 - y).wait_recv()
            c_copy(q, c, 1).start()

    step = 256 if total % 256 == 0 else total
    tile = 256 if hidden % 256 == 0 else LANES

    def first(q):
        c_copy(q, 1 - c, 0).wait_recv()
        if ny > 1:
            c_copy(q, 1 - c, 1).wait_recv()
        for copy in weights(q):
            copy.wait()
        for low in range(0, total, step):
            some = slice(low, low + step)

            @pl.loop(0, hidden // tile)
            def _(n):
                part = pl.ds(pl.multiple_of(n * tile, tile), tile)
                x = data[q, some, :cols]
                g = dot(x, gate_v[q, :, part])
                u = dot(x, up_v[q, :, part])
                d = dot_t(data[q, some, cols : 2 * cols], down_v[q, part, :])
                if q == 0:
                    gate[some, part] = g
                    upper[some, part] = u
                    dact[some, part] = d
                else:
                    gate[some, part] += g
                    upper[some, part] += u
                    dact[some, part] += d

    for q in range(min(LEAD, chunks)):
        begin(q)
    for slot in range(chunks + 2 * GAP + 1):
        if slot + LEAD < chunks:
            begin(slot + LEAD)
        if 0 <= slot - GAP < chunks:
            gather_across(slot - GAP)
        if slot < chunks:
            gather_z(slot)
        if 0 <= slot - 2 * GAP < chunks:
            first(slot - 2 * GAP)

    for q in range(chunks):
        for offset in range(1, nz):
            both(offset, lambda way, other: z_copy(q, way, offset, z, other).wait_send())
        if ny > 1:
            for block in range(nz):
                y_copy(q, block, y).wait_send()
            c_copy(q, c, 1).wait_send()
        c_copy(q, c, 0).wait_send()

    mine = me // (2 * ny * nz // EXPERTS)
    for low in range(0, total, step):
        some = slice(low, low + step)
        named = data[0, some, 2 * cols :].astype(F32)
        lanes = lax.broadcasted_iota(jnp.int32, named.shape, 1)
        share = jnp.sum(jnp.where(lanes == mine, named, 0.0), axis=1, keepdims=True)
        share = share / jnp.sum(named, axis=1, keepdims=True)

        @pl.loop(0, hidden // LANES)
        def _(n):
            part = pl.ds(pl.multiple_of(n * LANES, LANES), LANES)
            g = gate[some, part]
            u = upper[some, part]
            d = dact[some, part] * share
            sigma = jax.nn.sigmoid(g)
            silu = g * sigma
            act[some, part] = (silu * u * share).astype(BF16)
            dgate[some, part] = (d * u * sigma * (1.0 + g * (1.0 - sigma))).astype(BF16)
            dup[some, part] = (d * silu).astype(BF16)

    def a_copy(q):
        return remote(
            held(q, 1 - c, 0, 0, ny * nz, 2 * cols), from_core.at[q], a_s.at[q], a_r.at[q], sibling
        )

    def b_copy(q):
        return remote(
            held(q, c, ny - 1 - y, 0, nz, 2 * cols), from_y.at[q], b_s.at[q], b_r.at[q], across
        )

    def landing(q, source):
        return from_z.at[q, pl.ds(pl.multiple_of(source * rows, rows), rows), :]

    def p_copy(q, way, offset, block, source):
        return remote(
            held(q, c, y, block, 1, 2 * cols),
            landing(q, source),
            ps.at[q, way, offset - 1],
            pr.at[q, way, offset - 1],
            at(block, y, c),
        )

    wide = 256 if cols % 256 == 0 else LANES

    def second(q):
        for low in range(0, total, step):
            some = slice(low, low + step)

            @pl.loop(0, cols // wide)
            def _(n):
                start = pl.multiple_of(n * wide, wide)
                part = pl.ds(start, wide)
                out = dot(act[some, :], down_v[q, :, part])
                back = dot_t(dgate[some, :], gate_v[q, part, :])
                back = back + dot_t(dup[some, :], up_v[q, part, :])
                data[q, some, part] = out.astype(BF16)
                data[q, some, pl.ds(pl.multiple_of(cols + start, LANES), wide)] = back.astype(BF16)

        a_copy(q).start()

    def add(q, start, count, other):
        ref = data.at[q, pl.ds(start, count), pl.ds(0, 2 * cols)]
        ref[...] = (ref[...].astype(F32) + other.astype(F32)).astype(BF16)

    def sum_core(q):
        a_copy(q).wait_recv()
        if ny > 1:
            theirs = (ny - 1 - y) * nz * rows
            add(q, place(c, ny - 1 - y, 0), nz * rows, from_core[q, pl.ds(pl.multiple_of(theirs, rows), nz * rows), :])
            b_copy(q).start()
        add(q, place(c, y, 0), nz * rows, from_core[q, pl.ds(pl.multiple_of(y * nz * rows, rows), nz * rows), :])

    def sum_across(q):
        if ny > 1:
            b_copy(q).wait_recv()
            add(q, place(c, y, 0), nz * rows, from_y[q])
        for offset in range(1, nz):
            both(offset, lambda way, other: p_copy(q, way, offset, other, z).start())

    def sum_z(q):
        part = slice(q * 2 * cols, (q + 1) * 2 * cols)
        final[:, part] = held(q, c, y, z, 1, 2 * cols)[...].astype(F32)

        def arrived(way, offset, other):
            p_copy(q, 1 - way, offset, other, other).wait_recv()
            final[:, part] += landing(q, other)[...].astype(F32)

        for offset in range(1, nz):
            both(offset, lambda way, other: arrived(way, offset, other))

    for slot in range(chunks + 3 * GAP):
        if slot < chunks:
            second(slot)
        if 0 <= slot - 3 * GAP < chunks:
            sum_z(slot - 3 * GAP)
        if 0 <= slot - 2 * GAP < chunks:
            sum_across(slot - 2 * GAP)
        if 0 <= slot - GAP < chunks:
            sum_core(slot - GAP)

    for q in range(chunks):
        a_copy(q).wait_send()
        if ny > 1:
            b_copy(q).wait_send()
        for offset in range(1, nz):
            both(offset, lambda way, other: p_copy(q, way, offset, other, z).wait_send())

    values = tokens[...].astype(F32)
    scale = lax.rsqrt(jnp.mean(values * values, axis=-1, keepdims=True) + 1e-06)
    inner = jnp.zeros((rows, 1), F32)
    for q in range(chunks):
        part = slice(q * cols, (q + 1) * cols)
        mixed[:, part] = final[:, 2 * q * cols : (2 * q + 1) * cols].astype(BF16)
        scaled = final[:, (2 * q + 1) * cols : (2 * q + 2) * cols] * gain[:, part]
        final[:, (2 * q + 1) * cols : (2 * q + 2) * cols] = scaled
        inner = inner + jnp.sum(scaled * values[:, part], axis=-1, keepdims=True)
    inner = inner / width * scale * scale * scale
    for q in range(chunks):
        part = slice(q * cols, (q + 1) * cols)
        scaled = final[:, (2 * q + 1) * cols : (2 * q + 2) * cols]
        token_grad[:, part] = (scaled * scale - values[:, part] * inner).astype(BF16)


def local(nz, ny, tokens, norm_gain, gate_weight, up_weight, down_weight, routes, fractions, cotangent):
    rows, width = tokens.shape
    hidden = gate_weight.shape[1]
    chunks = max(1, 32 // nz)
    cols = width // chunks
    total = 2 * ny * nz * rows
    dma = pltpu.SemaphoreType.DMA
    in_vmem = pl.BlockSpec(memory_space=pltpu.VMEM)
    in_hbm = pl.BlockSpec(memory_space=pl.ANY)
    out = jax.ShapeDtypeStruct((rows, width), BF16)
    hops = max(1, nz - 1)
    return pl.pallas_call(
        functools.partial(kernel, nz, ny, chunks),
        out_shape=(out, out),
        in_specs=[in_vmem] * 5 + [in_hbm] * 3,
        out_specs=(in_vmem, in_vmem),
        scratch_shapes=[
            pltpu.VMEM((chunks, total, 2 * cols + LANES), BF16),
            pltpu.VMEM((chunks, cols, hidden), BF16),
            pltpu.VMEM((chunks, cols, hidden), BF16),
            pltpu.VMEM((chunks, hidden, cols), BF16),
            pltpu.VMEM((total, hidden), F32),
            pltpu.VMEM((total, hidden), F32),
            pltpu.VMEM((total, hidden), F32),
            pltpu.VMEM((total, hidden), BF16),
            pltpu.VMEM((total, hidden), BF16),
            pltpu.VMEM((total, hidden), BF16),
            pltpu.VMEM((chunks, total // 2, 2 * cols), BF16),
            pltpu.VMEM((chunks, nz * rows if ny > 1 else 16, 2 * cols), BF16),
            pltpu.VMEM((chunks, nz * rows, 2 * cols), BF16),
            pltpu.VMEM((rows, 2 * width), F32),
            dma((chunks, 3)),
            dma((chunks, 2, hops)),
            dma((chunks, 2, hops)),
            dma((chunks, nz)),
            dma((chunks, nz)),
            dma((chunks, 2)),
            dma((chunks, 2)),
            dma((chunks,)),
            dma((chunks,)),
            dma((chunks,)),
            dma((chunks,)),
            dma((chunks, 2, hops)),
            dma((chunks, 2, hops)),
        ],
        compiler_params=pltpu.CompilerParams(
            collective_id=0, has_side_effects=True, vmem_limit_bytes=62 * 1024 * 1024
        ),
        cost_estimate=pl.CostEstimate(
            flops=12 * total * width * hidden,
            bytes_accessed=6 * width * hidden,
            transcendentals=total * hidden,
        ),
    )(tokens, norm_gain.reshape(1, width), routes, fractions, cotangent, gate_weight, up_weight, down_weight)


def solution(mesh):
    rows = P(("grp", "exp"), None)
    placed = (rows, P(), P(None, "exp"), P(None, "exp"), P("exp", None), rows, rows, rows)
    ny = max(1, 4 // mesh.shape["grp"])
    nz = mesh.shape["exp"] // (2 * ny)
    return jax.shard_map(
        functools.partial(local, nz, ny),
        mesh=mesh,
        in_specs=placed,
        out_specs=(rows, rows),
        check_vma=False,
    )
```
